256 devices in a mesh: seq: 64 (over z, y, core), geo: 4 (over x).
Axes of the slice: x: 4, y: 4, z: 8, core: 2. Of those that a mesh axis runs over, the one named last changes fastest.
Arguments:
- ssm_input: bfloat16 [65536, 768], P(('geo', 'seq')), parts along dimension 0, may hold values from -6 to 6
- gate_input: bfloat16 [65536, 768], P(('geo', 'seq')), parts along dimension 0, may hold values from -6 to 6
- state_proj: bfloat16 [65536, 128], P(('geo', 'seq')), parts along dimension 0, may hold values from -6 to 6
- step_raw: float32 [12, 65536], P(None, ('geo', 'seq')), parts along dimension 1, may hold values from -5 to 5
- decay_log: float32 [12], replicated, may hold values from -20 to 2
- step_bias: float32 [12], replicated, may hold values from -8 to -3
- skip_gain: float32 [12], replicated, may hold values from 0.5 to 1.5
- norm_gain: float32 [768], replicated, may hold values from 0.25 to 1.75
- out_weight: bfloat16 [768, 384], replicated, may hold values from -0.21875 to 0.21875
- block_counts: int32 [256, 64], P('geo'), parts along dimension 0, may hold values from 0 to 2, as said below
- out_cotangent: bfloat16 [65536, 384], P(('geo', 'seq')), parts along dimension 0, may hold values from -6 to 6
Outputs:
- mixed_points: bfloat16 [65536, 384], P(('geo', 'seq')), parts along dimension 0
- grad_input: bfloat16 [65536, 768], P(('geo', 'seq')), parts along dimension 0
- grad_gate: bfloat16 [65536, 768], P(('geo', 'seq')), parts along dimension 0
- grad_proj: bfloat16 [65536, 128], P(('geo', 'seq')), parts along dimension 0
- grad_step: float32 [12, 65536], P(None, ('geo', 'seq')), parts along dimension 1
- grad_weight: float32 [3072, 384], P('geo'), parts along dimension 0
- grad_heads: float32 [12, 12], P('geo'), parts along dimension 0
- grad_norm: float32 [3072], P('geo'), parts along dimension 0
The draws below stay inside these ranges and needn't reach their ends.
There are 4 independent parts, one for each index of `geo`. The reference program is written for one: setup_inputs(seed, part) draws one part's arguments, and reference() takes and returns one part's arrays. A program takes and returns all parts, laid end to end along the dimension named above; an argument that names none is the same for every part. Nothing has to cross between parts.
Inputs may be any that keep to these rules, and one draw needn't show every extreme that they name: block_counts[s, t] is the number of aligned blocks of 128 rows that shard s sends to shard t: symmetric, zero unless s and t differ by at most one, each row sums to 2; entries off the diagonal are at most 1, reached in every draw; shards 0 and 1 exchange exactly 1 block each way.
All inputs are finite; a program needn't handle non-finite values.
Results may differ from the reference program's by a relative error of at most 0.0049.
Values may be sent and summed in bfloat16 or wider, within the bound.
A program may use at most 128 MiB of HBM per device.

```python
import jax
import jax.numpy as jnp
from jax import lax

D = 384
HEADS = 12
STATE = 64
ROWS_DEV = 256
BLOCK_ROWS = 128
GROUP = 256
DIN = 768
BLOCKS_DEV = 2
MOVE_MAX = 1
SHARDS = 64
POINTS = 16384


def head_rates(key):
    folded = jax.random.fold_in(key, 11)
    key_order, key_step, key_keep = jax.random.split(folded, 3)
    ranking = jax.random.permutation(key_order, HEADS)
    if HEADS >= 4:
        middle_quick = ranking == HEADS - 2
        middle_drawn = ranking == HEADS - 3
    else:
        middle_quick = ranking < 0
        middle_drawn = ranking < 0
    is_middle = middle_quick | middle_drawn
    is_slow = (ranking < (HEADS + 1) // 2) & ~is_middle
    fraction = jax.random.uniform(key_step, (HEADS,), jnp.float32)
    keeping = jax.random.uniform(key_keep, (HEADS,), jnp.float32)
    step_base = jnp.where(is_slow, 0.0005 * 4.0 ** fraction, 0.01 * 4.0 ** fraction)
    step_base = jnp.where(is_middle, 0.005 * 4.0 ** fraction, step_base)
    rate_slow = (0.3 + 1.2 * keeping) / (POINTS * 1.65 * step_base)
    rate_fast = 0.02 * 2.5 ** keeping / (1.65 * step_base)
    shard_loss = jnp.where(middle_quick, 0.5 + 0.5 * keeping, 0.2 + 0.15 * keeping)
    rate_middle = shard_loss / (ROWS_DEV * 1.65 * step_base)
    decay_rate = jnp.where(is_slow, rate_slow, rate_fast)
    decay_rate = jnp.where(is_middle, rate_middle, decay_rate)
    return (jnp.log(decay_rate), jnp.log(jnp.expm1(step_base)))


def draw_decay_log(key, part):
    return head_rates(key)[0]


def draw_step_bias(key, part):
    return head_rates(key)[1]


def draw_block_counts(key, part):
    folded = jax.random.fold_in(key, 23)
    key_moves, key_pick = jax.random.split(folded)
    shards = SHARDS
    move_counts = jax.random.randint(key_moves, (shards - 1,), 0, MOVE_MAX + 1, dtype=jnp.int32)
    chosen = jax.random.randint(key_pick, (), 1, shards - 1, dtype=jnp.int32)
    places = jnp.arange(shards - 1, dtype=jnp.int32)
    move_counts = jnp.where((places == 0) | (places == chosen), MOVE_MAX, move_counts)
    upward = jnp.concatenate([move_counts, jnp.zeros((1,), jnp.int32)])
    downward = jnp.concatenate([jnp.zeros((1,), jnp.int32), move_counts])
    row_ids = jnp.arange(shards, dtype=jnp.int32)[:, None]
    col_ids = jnp.arange(shards, dtype=jnp.int32)[None, :]
    counts = jnp.where(col_ids == row_ids + 1, upward[:, None], 0)
    counts = counts + jnp.where(col_ids == row_ids - 1, downward[:, None], 0)
    counts = counts + jnp.where(col_ids == row_ids, (BLOCKS_DEV - upward - downward)[:, None], 0)
    return counts.astype(jnp.int32)


def steps_of(stream_key, shape, cuts, low, high):
    factor_of, own = 1.0, jax.random.fold_in(stream_key, 6)
    for dim, blocks in cuts:
        heights = jnp.exp(jax.random.uniform(jax.random.fold_in(own, dim), (blocks,), jnp.float32, low / len(cuts), high / len(cuts)))
        factor_of = factor_of * jnp.repeat(heights, shape[dim] // blocks).reshape([-1 if axis == dim else 1 for axis in range(len(shape))])
    return factor_of


def noise(stream_key, shape, width, limit, cuts=(), held_as=jnp.bfloat16):
    entries = jax.random.normal(stream_key, shape, jnp.float32) * width
    if len(cuts) > 0:
        entries = steps_of(stream_key, shape, cuts, -0.22, 0.18) * entries
    return jnp.clip(entries, min=-limit, max=limit).astype(held_as)


def setup_inputs(seed: int = 0, part: int = 0) -> dict:
    streams_of = jax.random.split(jax.random.key(seed), 12)
    part_keys = jax.random.split(jax.random.fold_in(streams_of[11], part), 12)
    return {
        "ssm_input": noise(part_keys[0], (POINTS, DIN), 1.0, 6.0, ((0, 64),)),
        "gate_input": noise(part_keys[1], (POINTS, DIN), 1.0, 6.0, ((0, 64),)),
        "state_proj": noise(part_keys[2], (POINTS, 2 * STATE), 1.0, 6.0, ((0, 64),)),
        "step_raw": noise(part_keys[3], (HEADS, POINTS), 1.0, 5.0, ((1, 64),), jnp.float32),
        "decay_log": draw_decay_log(jax.random.fold_in(streams_of[11], 71), part),
        "step_bias": draw_step_bias(jax.random.fold_in(streams_of[11], 71), part),
        "skip_gain": jnp.clip(jax.random.uniform(streams_of[6], (HEADS,), jnp.float32, 0.5, 1.5), 0.5, 1.5),
        "norm_gain": jnp.clip(1.0 + 0.15 * jax.random.normal(streams_of[7], (DIN,), jnp.float32), 0.25, 1.75),
        "out_weight": noise(streams_of[8], (DIN, D), DIN ** -0.5, 0.21875),
        "block_counts": draw_block_counts(jax.random.fold_in(jax.random.fold_in(streams_of[11], part), 71), part),
        "out_cotangent": noise(part_keys[10], (POINTS, D), 1.0, 6.0, ((0, 64),)),
    }


highest = lax.Precision.HIGHEST

def step_decay(step_raw, decay_log, step_bias):
    step_size = jax.nn.softplus(step_raw + step_bias[:, None])
    log_decay = step_size * (-jnp.exp(decay_log))[:, None]
    return (step_size, log_decay)

def group_scan(state_now, pieces):
    x_group, b_group, c_group, step_group, decay_group = pieces
    cumulative = jnp.cumsum(decay_group, axis=1)
    length = cumulative.shape[1]
    lower_mask = (jnp.arange(length)[:, None] >= jnp.arange(length)[None, :])[None]
    spread = jnp.where(lower_mask, cumulative[:, :, None] - cumulative[:, None, :], 0.0)
    weights = jnp.where(lower_mask, jnp.exp(spread), 0.0)
    scores = jnp.dot(c_group, b_group.T, precision=highest)
    mixing = scores[None] * weights * step_group[:, None, :]
    y_local = jnp.einsum('hij,jhp->ihp', mixing, x_group, precision=highest)
    y_carry = jnp.einsum('in,hnp->ihp', c_group, state_now, precision=highest) * jnp.exp(cumulative).T[:, :, None]
    tail_weight = jnp.exp(cumulative[:, -1:] - cumulative) * step_group
    state_next = jnp.exp(cumulative[:, -1])[:, None, None] * state_now + jnp.einsum('hj,jn,jhp->hnp', tail_weight, b_group, x_group, precision=highest)
    return (state_next, y_local + y_carry)

def gated_norm(y_ssd, gate_f, norm_gain):
    mixed = y_ssd * jax.nn.silu(gate_f)
    inverse_rms = lax.rsqrt(lax.optimization_barrier(jnp.mean(mixed * mixed, axis=-1, keepdims=True)) + 1e-05)
    return mixed * inverse_rms * norm_gain

def forward_all(ssm_f, gate_f, proj_f, step_raw, decay_log, step_bias, skip_gain, norm_gain):
    total_rows, row_width = ssm_f.shape
    head_count = decay_log.shape[0]
    head_dim = row_width // head_count
    state_dim = proj_f.shape[1] // 2
    step_size, log_decay = step_decay(step_raw, decay_log, step_bias)
    groups = total_rows // GROUP
    x_all = ssm_f.reshape(groups, GROUP, head_count, head_dim)
    b_all = proj_f[:, :state_dim].reshape(groups, GROUP, state_dim)
    c_all = proj_f[:, state_dim:].reshape(groups, GROUP, state_dim)
    step_all = step_size.reshape(head_count, groups, GROUP).transpose(1, 0, 2)
    decay_all = log_decay.reshape(head_count, groups, GROUP).transpose(1, 0, 2)
    zero_state = jnp.zeros((head_count, state_dim, head_dim), jnp.float32)
    _, y_all = lax.scan(jax.checkpoint(group_scan), zero_state, (x_all, b_all, c_all, step_all, decay_all))
    y_ssd = y_all.reshape(total_rows, row_width) + ssm_f * jnp.repeat(skip_gain, head_dim)[None, :]
    return gated_norm(y_ssd, gate_f, norm_gain)

def regroup_order(block_counts, blocks_dev):
    shards = block_counts.shape[0]
    upper_counts = jnp.concatenate([jnp.diagonal(block_counts, 1), jnp.zeros((1,), jnp.int32)]).astype(jnp.int32)
    lower_counts = jnp.concatenate([jnp.zeros((1,), jnp.int32), jnp.diagonal(block_counts, -1)]).astype(jnp.int32)
    target = jnp.arange(shards * blocks_dev, dtype=jnp.int32)
    shard_of = target // blocks_dev
    within = target % blocks_dev
    before_count = lower_counts[shard_of]
    after_count = upper_counts[shard_of]
    shift = jnp.where(within < before_count, -before_count, jnp.where(within >= blocks_dev - after_count, after_count, 0))
    return (target + shift).astype(jnp.int32)

def regroup(row_data, block_ids):
    blocks = row_data.reshape(block_ids.shape[0], BLOCK_ROWS, -1)
    return blocks[block_ids].reshape(row_data.shape)

def reference(ssm_input, gate_input, state_proj, step_raw, decay_log, step_bias, skip_gain, norm_gain, out_weight, block_counts, out_cotangent):
    ssm_f = ssm_input.astype(jnp.float32)
    gate_f = gate_input.astype(jnp.float32)
    proj_f = state_proj.astype(jnp.float32)
    normed_f, pullback = jax.vjp(forward_all, ssm_f, gate_f, proj_f, step_raw, decay_log, step_bias, skip_gain, norm_gain)
    normed = normed_f.astype(jnp.bfloat16)
    block_ids = regroup_order(block_counts, BLOCKS_DEV)
    out_rows = jnp.dot(normed, out_weight, preferred_element_type=jnp.float32).astype(jnp.bfloat16)
    mixed_points = regroup(out_rows, block_ids)
    returned = regroup(out_cotangent, block_ids)
    g_normed = jnp.dot(returned, out_weight.T, preferred_element_type=jnp.float32)
    grad_scale = POINTS ** (-0.5)
    grad_weight = jnp.dot(normed.T, returned, preferred_element_type=jnp.float32) * grad_scale
    cotangents = pullback(g_normed)
    grad_heads = jnp.stack([cotangents[4], cotangents[5], cotangents[6]]) * grad_scale
    grad_norm = cotangents[7] * grad_scale
    return (mixed_points, cotangents[0].astype(jnp.bfloat16), cotangents[1].astype(jnp.bfloat16), cotangents[2].astype(jnp.bfloat16), cotangents[3], grad_weight, grad_heads, grad_norm)
```

```python
import functools

import jax
import jax.numpy as jnp
from jax import lax
from jax.experimental import pallas as pl
from jax.experimental.pallas import tpu as pltpu
from jax.sharding import PartitionSpec as P

ROWS = 256
HEADS = 12
DIN = 768
WIDTH = 384
BLOCK = 128
PLANE = 8
TILES = DIN // 128
f32 = jnp.float32
bf16 = jnp.bfloat16
MESH = pl.DeviceIdType.MESH

FA, FB, FC, BA, BB, BC, RC, RO, W1, W2, W3, W4, W5, W6, HA, HB = range(16)


def mm(a, b):
    return jnp.dot(a, b, preferred_element_type=f32)


def mmt(a, b):
    return lax.dot_general(a, b, (((1,), (1,)), ((), ())), preferred_element_type=f32)


def iota(shape, dim):
    return lax.broadcasted_iota(jnp.int32, shape, dim)


def split2(v):
    hi = v.astype(bf16)
    return hi, (v - hi.astype(f32)).astype(bf16)


def split3(v):
    hi = v.astype(bf16)
    rest = v - hi.astype(f32)
    mid = rest.astype(bf16)
    return hi, mid, (rest - mid.astype(f32)).astype(bf16)


def running(v, ones):
    r = mm(jnp.concatenate(split3(v), axis=0), ones)
    return r[0:16] + r[16:32] + r[32:48]


def softplus(v):
    u = jnp.exp(-jnp.abs(v))
    series = u * (1 - u * (1 / 2 - u * (1 / 3 - u * (1 / 4 - u * (1 / 5 - u * (1 / 6))))))
    return jnp.maximum(v, 0.0) + jnp.where(u < 0.05, series, jnp.log(1 + u))


def kernel(
    nz,
    scale,
    x_ref,
    z_ref,
    bc_ref,
    raw_ref,
    dlog_ref,
    bias_ref,
    skip_ref,
    gain_ref,
    w_ref,
    cnt_ref,
    cot_ref,
    mixed_ref,
    gx_ref,
    gz_ref,
    gp_ref,
    gs_ref,
    gw_ref,
    gh_ref,
    gn_ref,
    pad,
    prow,
    trow,
    colt,
    e768,
    t768,
    txh,
    txl,
    bct,
    swt,
    sc,
    wst,
    mix,
    mixt,
    xm,
    yl,
    sg,
    sgh,
    sgl,
    ret,
    gnorm,
    tmp,
    normed,
    normt,
    gy,
    gb,
    g3h,
    g3l,
    ph,
    plo,
    dsc,
    dsct,
    dxl,
    gpl,
    acc,
    orow,
    wt,
    fa_s,
    fa_r,
    fb_s,
    fb_r,
    fc_s,
    fc_r,
    ba_s,
    ba_r,
    bb_s,
    bb_r,
    bc_s,
    bc_r,
    ent,
    dpre,
    rprev,
    rnext,
    oprev,
    onext,
    w1s,
    w1r,
    w2s,
    w2r,
    w3s,
    w3r,
    w4s,
    w4r,
    w5r,
    w6r,
    ha_s,
    ha_r,
    hb_s,
    hb_r,
    ssem,
    rsem,
):
    shards = PLANE * nz
    nred = w4r.shape[0]
    s = lax.axis_index("seq")
    zi, k = s // PLANE, s % PLANE
    yi, ci = k // 2, k % 2

    barrier = pltpu.get_barrier_semaphore()

    def greet(i):
        pl.semaphore_signal(barrier, inc=1, device_id={"seq": i}, device_id_type=MESH)

    for d in range(1, PLANE):
        greet(zi * PLANE + (k + d) % PLANE)
    for d in range(1, nz):
        greet(((zi + d) % nz) * PLANE + k)
    greet((s + 1) % shards)
    greet((s + shards - 1) % shards)

    def copy(src, dst, phase, d, i):
        return pltpu.make_async_remote_copy(
            src_ref=src,
            dst_ref=dst,
            send_sem=ssem.at[phase, d],
            recv_sem=rsem.at[phase, d],
            device_id={"seq": i},
            device_id_type=MESH,
        )

    def plane_copies(src, dst, phase):
        peers = [(k + d) % PLANE for d in range(1, PLANE)]
        return [
            copy(src(p), dst, phase, d + 1, zi * PLANE + p) for d, p in enumerate(peers)
        ]

    def z_copies(src, dst, phase):
        peers = [(zi + d) % nz for d in range(1, nz)]
        return [copy(src(p), dst, phase, d + 1, p * PLANE + k) for d, p in enumerate(peers)]

    def start(copies):
        for c in copies:
            c.start()

    def wait(copies):
        for c in copies:
            c.wait()

    def state_out(state, send, recv, phase):
        for j in range(PLANE):
            for c in range(TILES):
                send[j, c] = state[8 * j : 8 * j + 8, 128 * c : 128 * c + 128]
        for c in range(TILES):
            prow[c : c + 1, :] = e768[ROWS - 1 : ROWS, 128 * c : 128 * c + 128]
        for j in range(PLANE):
            send[j, TILES] = prow[...]
        recv[k] = send[k]
        copies = plane_copies(lambda p: send.at[p], recv.at[k], phase)
        start(copies)
        return copies

    def scan_plane(recv, send, zrecv, order, phase):
        dp = jnp.ones((8, 128), f32)
        total = [jnp.zeros((8, 128), f32)] * TILES
        for j in order:
            dt = recv[j, TILES]
            dpre[j] = dp
            for c in range(TILES):
                ent[j, c] = total[c]
                total[c] = dt[c : c + 1, :] * total[c] + recv[j, c]
            dp = dp * dt
        for c in range(TILES):
            send[c] = total[c]
        send[TILES] = dp
        zrecv[zi] = send[...]
        copies = z_copies(lambda p: send, zrecv.at[zi], phase)
        start(copies)
        return copies

    def scan_z(zrecv, send, recv, order, takes, phase):
        total = [jnp.zeros((8, 128), f32)] * TILES
        for j in order:
            dt = zrecv[j, TILES]
            use = takes(j)
            for c in range(TILES):
                longer = dt[c : c + 1, :] * total[c] + zrecv[j, c]
                total[c] = jnp.where(use, longer, total[c])
        for j in range(PLANE):
            dp = dpre[j]
            for c in range(TILES):
                send[j, c] = ent[j, c] + dp[c : c + 1, :] * total[c]
        recv[k] = send[k]
        copies = plane_copies(lambda p: send.at[p], recv.at[k], phase)
        start(copies)
        return copies

    def state_in(recv, first):
        for j in range(PLANE):
            for c in range(TILES):
                sg[first + 8 * j : first + 8 * j + 8, 128 * c : 128 * c + 128] = recv[j, c]
        half = pl.ds(first, 64)
        hi, lo = split2(sg[half, :])
        sgh[half, :] = hi
        sgl[half, :] = lo

    head_lane = iota((16, 128), 0) == iota((16, 128), 1)
    prow[...] = jnp.ones((8, 128), f32)
    trow[...] = jnp.zeros((128, ROWS), f32)
    trow[0:1, 0:HEADS] = dlog_ref[...]
    trow[8:9, 0:HEADS] = bias_ref[...]
    trow[16:17, 0:HEADS] = skip_ref[...]
    pad[...] = jnp.zeros((16, ROWS), f32)
    pad[0:HEADS, :] = raw_ref[...]

    def as_column(i):
        return jnp.sum(jnp.where(head_lane, trow[i : i + 1, 0:128], 0.0), axis=1, keepdims=True)

    rate = jnp.exp(as_column(0))
    shifted = pad[...] + as_column(8)
    skip_col = as_column(16)
    owns = iota((16, DIN), 1) // 64 == iota((16, DIN), 0)
    skip_row = jnp.sum(jnp.where(owns, skip_col, 0.0), axis=0, keepdims=True)
    step = softplus(shifted)
    log_decay = -rate * step
    upper = (iota((ROWS, ROWS), 0) <= iota((ROWS, ROWS), 1)).astype(bf16)
    cum = running(log_decay, upper)
    ecum = jnp.exp(cum)
    tail = jnp.exp(cum[:, ROWS - 1 : ROWS] - cum) * step
    pad[...] = step
    trow[0:16, :] = cum
    for first, value in ((16, ecum), (64, tail)):
        for i, part in enumerate(split3(value)):
            trow[first + 16 * i : first + 16 * i + 16, :] = part.astype(f32)
    trow[112:128, :] = jnp.zeros((16, ROWS), f32)
    columns = trow[...].T
    colt[...] = columns
    parts = columns.astype(bf16)
    row_id = iota((128, DIN), 0)
    mine = iota((128, DIN), 1) // 64 == row_id % 16
    e768[...] = mm(parts, (mine & (row_id >= 16) & (row_id < 64)).astype(bf16))
    t768[...] = mm(parts, (mine & (row_id >= 64) & (row_id < 112)).astype(bf16))

    bcf = bc_ref[...].astype(f32)
    bct[...] = bcf.T.astype(bf16)
    lane = iota((ROWS, 128), 1)
    bc_b = jnp.where(lane < 64, bcf, 0.0).astype(bf16)
    bc_c = jnp.where(lane < 64, 0.0, bcf).astype(bf16)

    @pl.loop(0, ROWS // 32)
    def _(i):
        rows = pl.ds(pl.multiple_of(i * 32, 32), 32)
        hi, lo = split2(t768[rows, :] * x_ref[rows, :].astype(f32))
        txh[rows, :] = hi
        txl[rows, :] = lo

    local_state = mm(bct[0:64, :], txh[...]) + mm(bct[0:64, :], txl[...])

    pl.semaphore_wait(barrier, (PLANE - 1) + (nz - 1) + 2)
    fa = state_out(local_state, fa_s, fa_r, FA)
    rc = [
        copy(cot_ref.at[pl.ds(BLOCK, BLOCK), :], rprev, RC, 0, (s + 1) % shards),
        copy(cot_ref.at[pl.ds(0, BLOCK), :], rnext, RC, 1, (s + shards - 1) % shards),
    ]
    start(rc)

    swt[0:64, :] = bct[64:128, :]
    swt[64:128, :] = bct[0:64, :]
    sc[...] = mm(bc_c, swt[...])

    cum_now = trow

    @pl.loop(0, ROWS // 64)
    def _(i):
        first = pl.multiple_of(i * 64, 64)
        rows = pl.ds(first, 64)
        keep = iota((64, ROWS), 0) + first >= iota((64, ROWS), 1)
        score = sc[rows, :]
        col = colt[rows, :]
        for h in range(HEADS):
            spread = col[:, h : h + 1] - cum_now[h : h + 1, :]
            weight = jnp.where(keep, jnp.exp(spread), 0.0) * pad[h : h + 1, :]
            wst[h, rows, :] = weight.astype(bf16)
            mix[h, rows, :] = (weight * score).astype(bf16)

    wait(fa)
    fb = scan_plane(fa_r, fb_s, fb_r, range(PLANE), FB)

    @pl.loop(0, TILES)
    def _(i):
        cols = pl.ds(pl.multiple_of(i * 128, 128), 128)
        both = x_ref[:, cols].astype(f32)
        xm[2 * i] = jnp.where(lane < 64, both, 0.0).astype(bf16)
        xm[2 * i + 1] = jnp.where(lane < 64, 0.0, both).astype(bf16)
        yl[:, cols] = mm(mix[2 * i], xm[2 * i]) + mm(mix[2 * i + 1], xm[2 * i + 1])

    wait(fb)
    fc = scan_z(fb_r, fc_s, fc_r, range(nz), lambda j: j < zi, FC)

    wait(rc)
    count_row = iota(cnt_ref.shape, 0) == s
    count_col = iota(cnt_ref.shape, 1)

    def count(col):
        here = jnp.where(count_row & (count_col == col), cnt_ref[...], 0).astype(f32)
        return jnp.sum(jnp.sum(here, axis=1, keepdims=True), axis=0, keepdims=True)

    from_prev = jnp.broadcast_to(count(s - 1), (BLOCK, WIDTH)) > 0.0
    from_next = jnp.broadcast_to(count(s + 1), (BLOCK, WIDTH)) > 0.0

    def regroup(out, own, prev, following):
        upper_half, lower_half = pl.ds(0, BLOCK), pl.ds(BLOCK, BLOCK)
        out[upper_half, :] = jnp.where(
            from_prev, prev[...].astype(f32), own[upper_half, :].astype(f32)
        ).astype(bf16)
        out[lower_half, :] = jnp.where(
            from_next, following[...].astype(f32), own[lower_half, :].astype(f32)
        ).astype(bf16)

    regroup(ret, cot_ref, rprev, rnext)
    gnorm[...] = mmt(ret[...], w_ref[...])

    @pl.loop(0, HEADS)
    def _(h):
        mixt[h] = mix[h].astype(f32).T.astype(bf16)

    sg[0:64, :] = jnp.zeros((64, DIN), f32)
    sgh[0:64, :] = jnp.zeros((64, DIN), bf16)
    sgl[0:64, :] = jnp.zeros((64, DIN), bf16)
    acc[...] = jnp.zeros(acc.shape, f32)
    gain = gain_ref[...]

    wait(fc)
    state_in(fc_r, 64)
    tmp[...] = mm(bc_c, sgh[...]) + mm(bc_c, sgl[...])

    def by_eight(v):
        return sum(v[8 * i : 8 * i + 8] for i in range(v.shape[0] // 8))

    @pl.loop(0, ROWS // 16)
    def _(i):
        rows = pl.ds(pl.multiple_of(i * 16, 16), 16)
        x = x_ref[rows, :].astype(f32)
        z = z_ref[rows, :].astype(f32)
        local = yl[rows, :]
        reach = e768[rows, :]
        carried = tmp[rows, :]
        y = local + reach * carried + skip_row * x
        sig = 1.0 / (1.0 + jnp.exp(-z))
        silu = z * sig
        u = y * silu
        inv = lax.rsqrt(jnp.mean(u * u, axis=1, keepdims=True) + 1e-5)
        un = u * inv
        normed[rows, :] = (un * gain).astype(bf16)
        g = gnorm[rows, :]
        gg = g * gain
        gu = inv * (gg - un * jnp.mean(gg * un, axis=1, keepdims=True))
        gyv = gu * silu
        gz_ref[rows, :] = (gu * y * (sig * (1.0 + z * (1.0 - sig)))).astype(bf16)
        gyb = gyv.astype(bf16)
        gy[rows, :] = gyv
        gb[rows, :] = gyb
        g3 = gyv * reach
        hi, lo = split2(g3)
        g3h[rows, :] = hi
        g3l[rows, :] = lo
        hi, lo = split2(gyb.astype(f32) * local + g3 * carried)
        ph[rows, :] = hi
        plo[rows, :] = lo
        acc[0:8, :] += by_eight(g * un)
        acc[8:16, :] += by_eight(gyv * x)

    back_local = mm(bct[64:128, :], g3h[...]) + mm(bct[64:128, :], g3l[...])
    ba = state_out(back_local, ba_s, ba_r, BA)

    normt[...] = normed[...].astype(f32).T.astype(bf16)
    twin = zi * PLANE + yi * 2 + (1 - ci)
    theirs = pl.ds(pl.multiple_of((1 - ci) * WIDTH, WIDTH), WIDTH)
    ours = pl.ds(pl.multiple_of(ci * WIDTH, WIDTH), WIDTH)
    w1s[...] = mm(normt[theirs, :], ret[...]).astype(bf16)
    w1 = copy(w1s, w1r, W1, 0, twin)
    w1.start()
    orow[...] = mm(normed[...], w_ref[...]).astype(bf16)
    ro = [
        copy(orow.at[pl.ds(BLOCK, BLOCK), :], oprev, RO, 0, (s + 1) % shards),
        copy(orow.at[pl.ds(0, BLOCK), :], onext, RO, 1, (s + shards - 1) % shards),
    ]
    start(ro)
    wt[...] = mm(normt[ours, :], ret[...])

    wait(ba)
    bb = scan_plane(ba_r, bb_s, bb_r, range(PLANE - 1, -1, -1), BB)

    w1.wait()
    part = WIDTH // 4
    for j in range(4):
        rows = pl.ds(part * j, part)
        w2s[j] = (wt[rows, :] + w1r[rows, :].astype(f32)).astype(bf16)
    w2r[yi] = w2s[yi]
    y_peers = [(yi + d) % 4 for d in range(1, 4)]
    w2 = [
        copy(w2s.at[p], w2r.at[yi], W2, d, zi * PLANE + p * 2 + ci) for d, p in enumerate(y_peers)
    ]
    start(w2)

    @pl.loop(0, ROWS // 64)
    def _(i):
        rows = pl.ds(pl.multiple_of(i * 64, 64), 64)
        total = jnp.zeros((64, ROWS), f32)
        for h in range(HEADS):
            cols = pl.ds(128 * (h // 2), 128)
            total += mmt(gb[rows, cols], xm[h]) * wst[h, rows, :].astype(f32)
        dsc[rows, :] = total

    wait(bb)
    bcx = scan_z(bb_r, bc_s, bc_r, range(nz - 1, -1, -1), lambda j: j > zi, BC)

    @pl.loop(0, TILES)
    def _(i):
        cols = pl.ds(pl.multiple_of(i * 128, 128), 128)
        both = gb[:, cols].astype(f32)
        one = jnp.where(lane < 64, both, 0.0).astype(bf16)
        two = jnp.where(lane < 64, 0.0, both).astype(bf16)
        dxl[:, cols] = mm(mixt[2 * i], one) + mm(mixt[2 * i + 1], two)

    wait(w2)
    rows_z = part // nred
    for j in range(nred):
        rows = pl.ds(rows_z * j, rows_z)
        w3s[j] = sum(w2r[i, rows, :].astype(f32) for i in range(4)).astype(bf16)
    w3 = z_copies(lambda p: w3s.at[p], w3r.at[zi], W3)
    z_peers = [(zi + d) % nz for d in range(1, nz)]
    z_from = [(zi + nz - d) % nz for d in range(1, nz)]
    for c, p in zip(w3, z_peers):

        @pl.when(p < nred)
        def _(c=c):
            c.start()

    swapped = swt[...].astype(f32).T.astype(bf16)
    dsct[...] = dsc[...].T
    dh, dl = split2(dsc[...])
    th, tl = split2(dsct[...])
    gpl[...] = jnp.where(
        lane < 64, mm(th, swapped) + mm(tl, swapped), mm(dh, swapped) + mm(dl, swapped)
    )
    wait(ro)
    regroup(mixed_ref, orow, oprev, onext)

    for c, p in zip(w3, z_peers):

        @pl.when(p < nred)
        def _(c=c):
            c.wait_send()

    w4 = z_copies(lambda p: w4s, w4r.at[zi % nred], W4)

    @pl.when(zi < nred)
    def _():
        for c in w3:
            c.wait_recv()
        w3r[zi] = w3s[zi]
        whole = sum(w3r[i].astype(f32) for i in range(nz)).astype(bf16)
        w4s[...] = whole
        w4r[zi % nred] = whole
        start(w4)

    wait(bcx)
    state_in(bc_r, 0)
    tmp[...] = mm(bc_b, sgh[...]) + mm(bc_b, sgl[...])

    @pl.loop(0, ROWS // 16)
    def _(i):
        rows = pl.ds(pl.multiple_of(i * 16, 16), 16)
        x = x_ref[rows, :].astype(f32)
        far = t768[rows, :] * tmp[rows, :]
        dx = dxl[rows, :] + far
        gx_ref[rows, :] = (dx + skip_row * gy[rows, :]).astype(bf16)
        hi, lo = split2(x * dx)
        txl[rows, :] = hi
        g3l[rows, :] = lo
        acc[16:24, :] += by_eight(x * far)

    select = owns.astype(bf16)
    row_sum = mmt(select, ph[...]) + mmt(select, plo[...])
    col_sum = mmt(select, txl[...]) + mmt(select, g3l[...])

    def per_head(v):
        row = jnp.sum(v, axis=0, keepdims=True)
        return jnp.sum(jnp.where(owns, row, 0.0), axis=1, keepdims=True)

    meet = by_eight(sg[0:64, :] * sg[64:128, :]) * e768[ROWS - 1 : ROWS, :]
    last = per_head(acc[16:24, :] + meet)
    lower = (iota((ROWS, ROWS), 0) >= iota((ROWS, ROWS), 1)).astype(bf16)
    g_log = running(row_sum - col_sum, lower) + last
    g_raw = (col_sum / step - rate * g_log) / (1.0 + jnp.exp(-shifted))
    pad[...] = g_raw
    gs_ref[...] = pad[0:HEADS, :]

    def as_row(col):
        return jnp.sum(jnp.where(head_lane, col, 0.0), axis=0, keepdims=True)

    ha_s[...] = jnp.zeros((16, 128), f32)
    gain_sum = jnp.sum(acc[0:8, :], axis=0, keepdims=True)
    for c in range(TILES):
        ha_s[c : c + 1, :] = gain_sum[:, 128 * c : 128 * c + 128]
    ha_s[8:9, :] = as_row(jnp.sum(g_log * log_decay, axis=1, keepdims=True))
    ha_s[9:10, :] = as_row(jnp.sum(g_raw, axis=1, keepdims=True))
    ha_s[10:11, :] = as_row(per_head(acc[8:16, :]))
    ha_r[k] = ha_s[...]
    ha = plane_copies(lambda p: ha_s, ha_r.at[k], HA)
    start(ha)

    from_t = mmt(txh[...], sgh[...])
    from_g = mmt(g3h[...], sgh[...])
    gp_ref[...] = (gpl[...] + jnp.where(lane < 64, from_t, from_g)).astype(bf16)

    for c, p in zip(w4, z_from):

        @pl.when(p < nred)
        def _(c=c):
            c.wait_recv()

    w5r[yi] = w4r[...]
    w5 = [
        copy(w4r, w5r.at[yi], W5, d, zi * PLANE + p * 2 + ci) for d, p in enumerate(y_peers)
    ]
    start(w5)

    wait(ha)
    hb_s[...] = sum(ha_r[i] for i in range(PLANE))
    hb_r[zi] = hb_s[...]
    hb = z_copies(lambda p: hb_s, hb_r.at[zi], HB)
    start(hb)

    wait(w5)
    w6 = copy(w5r, w6r, W6, 0, twin)
    w6.start()

    def place(first, from_ref):
        for j in range(4):
            for i in range(nred):
                at = pl.multiple_of(first + part * j + rows_z * i, 16)
                gw_ref[pl.ds(at, rows_z), :] = from_ref[j, i].astype(f32) * scale

    place(ci * WIDTH, w5r)
    wait(hb)
    heads = sum(hb_r[i] for i in range(nz)) * scale
    gn_ref[...] = heads[0:TILES, :]
    gh_ref[...] = heads[8:11, 0:HEADS]
    w6.wait()
    place((1 - ci) * WIDTH, w6r)

    @pl.when(zi < nred)
    def _():
        for c in w4:
            c.wait_send()


def body(*args):
    shards = lax.axis_size("seq")
    nz = shards // PLANE
    nred = max(r for r in (1, 2, 3, 6) if r <= nz)
    rows_z = WIDTH // 4 // nred
    ssm, gate, proj, raw, dlog, bias, skip, gain, weight, counts, cot = args
    slots = (PLANE, TILES + 1, 8, 128)
    out = (PLANE, TILES, 8, 128)
    zslots = (nz, TILES + 1, 8, 128)

    def v(shape, dtype):
        return pltpu.VMEM(shape, dtype)

    big, bigh = v((ROWS, DIN), f32), v((ROWS, DIN), bf16)
    square = v((HEADS, ROWS, ROWS), bf16)
    scan = [
        v(slots, f32),
        v(slots, f32),
        v(slots[1:], f32),
        v(zslots, f32),
        v(out, f32),
        v(out, f32),
    ]
    block = v((BLOCK, WIDTH), bf16)
    scratch = [
        v((16, ROWS), f32),
        v((8, 128), f32),
        v((128, ROWS), f32),
        v((ROWS, 128), f32),
        big,
        big,
        bigh,
        bigh,
        v((128, ROWS), bf16),
        v((128, ROWS), bf16),
        v((ROWS, ROWS), f32),
        square,
        square,
        square,
        v((HEADS, ROWS, 128), bf16),
        big,
        v((128, DIN), f32),
        v((128, DIN), bf16),
        v((128, DIN), bf16),
        v((ROWS, WIDTH), bf16),
        big,
        big,
        bigh,
        v((DIN, ROWS), bf16),
        big,
        bigh,
        bigh,
        bigh,
        bigh,
        bigh,
        v((ROWS, ROWS), f32),
        v((ROWS, ROWS), f32),
        big,
        v((ROWS, 128), f32),
        v((24, DIN), f32),
        v((ROWS, WIDTH), bf16),
        v((WIDTH, WIDTH), f32),
        *scan,
        *scan,
        v(out, f32),
        v((PLANE, 8, 128), f32),
        block,
        block,
        block,
        block,
        v((WIDTH, WIDTH), bf16),
        v((WIDTH, WIDTH), bf16),
        v((4, WIDTH // 4, WIDTH), bf16),
        v((4, WIDTH // 4, WIDTH), bf16),
        v((nz, rows_z, WIDTH), bf16),
        v((nz, rows_z, WIDTH), bf16),
        v((rows_z, WIDTH), bf16),
        v((nred, rows_z, WIDTH), bf16),
        v((4, nred, rows_z, WIDTH), bf16),
        v((4, nred, rows_z, WIDTH), bf16),
        v((16, 128), f32),
        v((PLANE, 16, 128), f32),
        v((16, 128), f32),
        v((nz, 16, 128), f32),
        pltpu.SemaphoreType.DMA((16, 8)),
        pltpu.SemaphoreType.DMA((16, 8)),
    ]
    shape = jax.ShapeDtypeStruct
    results = pl.pallas_call(
        functools.partial(kernel, nz, float(ROWS * shards) ** -0.5),
        out_shape=(
            shape((ROWS, WIDTH), bf16),
            shape((ROWS, DIN), bf16),
            shape((ROWS, DIN), bf16),
            shape((ROWS, 128), bf16),
            shape((HEADS, ROWS), f32),
            shape((DIN, WIDTH), f32),
            shape((3, HEADS), f32),
            shape((TILES, 128), f32),
        ),
        in_specs=[pl.BlockSpec(memory_space=pltpu.VMEM)] * 11,
        out_specs=[pl.BlockSpec(memory_space=pltpu.VMEM)] * 8,
        scratch_shapes=scratch,
        compiler_params=pltpu.CompilerParams(
            collective_id=0, has_side_effects=True, vmem_limit_bytes=48 * 2**20
        ),
    )(
        ssm,
        gate,
        proj,
        raw,
        dlog.reshape(1, HEADS),
        bias.reshape(1, HEADS),
        skip.reshape(1, HEADS),
        gain.reshape(1, DIN),
        weight,
        counts,
        cot,
    )
    return (*results[:7], results[7].reshape(DIN))


def solution(mesh):
    rows = P(("geo", "seq"), None)
    cols = P(None, ("geo", "seq"))
    return jax.shard_map(
        body,
        mesh=mesh,
        in_specs=(rows, rows, rows, cols, P(), P(), P(), P(), P(), P("geo", None), rows),
        out_specs=(rows, rows, rows, rows, cols, P("geo", None), P("geo", None), P("geo")),
        check_vma=False,
    )
```
